128 devices in a mesh: seq: 16 (over y, z_hi, core), tp: 8 (over z_lo, x).
Axes of the slice: x: 4, y: 4, z: 4 (z_hi: 2, z_lo: 2; z = z_hi * 2 + z_lo), core: 2. Of those that a mesh axis runs over, the one named last changes fastest.
Arguments:
- teacher_rows: bfloat16 [8, 2048, 8192], P(None, 'seq', 'tp'), may hold values from -500 to 500
- projection: bfloat16 [8192, 2048], P('tp'), may hold values from -0.0625 to 0.0625
- queries: bfloat16 [8, 2048, 2048], P('tp', 'seq'), may hold values from -150 to 150
- cache_kv: bfloat16 [8, 4096, 2, 512], P('tp', 'seq'), may hold values from -6 to 6
- first_key: int32 [8, 16], P('tp', 'seq'), may hold values from 0 to 2048
- out_weight: bfloat16 [2048, 2048], replicated, may hold values from -0.125 to 0.125
Outputs:
- predicted: bfloat16 [8, 2048, 2048], P('tp', 'seq')
- grad_queries: float32 [8, 2048, 2048], P('tp', 'seq')
The draws below stay inside these ranges and needn't reach their ends.
Inputs may be any that keep to these rules, and one draw needn't show every extreme that they name: `first_key`: no query block starts its visible keys after the span's first position.
All inputs are finite; a program needn't handle non-finite values.
Results may differ from the reference program's by a relative error of at most 0.023.
Values may be sent and summed in bfloat16 or wider, within the bound.
No kernel may reach another device: no remote copies, remote signals or barrier semaphores. Data moves between devices by JAX's collectives and lax.ppermute only.
A program may use at most 128 MiB of HBM per device.

```python
import math
import jax
import jax.numpy as jnp
from jax import lax

DT = 8192
DS = 2048
QH = 16
KVH = 4
HD = 128
QBLOCK = 128
REPL = 8
SPAN = 2048
CACHE = 4096
N_TP = 8


def span_keys(key):
    normal_keys = jax.random.normal(key, (REPL, SPAN, KVH * HD), jnp.float32)
    return jnp.clip(normal_keys, -4.0, 4.0)


def draw_cache_kv(key, part):
    shared = span_keys(key)
    key = jax.random.fold_in(key, 11)
    key_early, key_values = jax.random.split(key, 2)
    early = jnp.clip(jax.random.normal(key_early, (REPL, CACHE - SPAN, KVH * HD), jnp.float32), -4.0, 4.0)
    keys_all = jnp.concatenate([early, shared], axis=1)
    values_all = jnp.clip(jax.random.normal(key_values, (REPL, CACHE, KVH * HD), jnp.float32), -4.0, 4.0)
    return jnp.stack([keys_all, values_all], axis=2).astype(jnp.bfloat16)


def draw_queries(key, part):
    key = jax.random.fold_in(key, 23)
    key_base = jax.random.fold_in(key, 0)
    base = jnp.clip(jax.random.normal(key_base, (REPL, SPAN, QH, HD), jnp.float32), -5.0, 5.0)
    return base.reshape(REPL, SPAN, QH * HD).astype(jnp.bfloat16)


def draw_teacher_rows(key, part):
    key = jax.random.fold_in(key, 37)
    key_base, key_rows = jax.random.split(key, 2)
    ramp = 10.0 ** (jnp.arange(DT, dtype=jnp.float32) / DT)
    row_scale = jnp.exp(jax.random.uniform(key_rows, (REPL, SPAN, 1), jnp.float32, 0.0, math.log(10.0)))
    base = jnp.clip(jax.random.normal(key_base, (REPL, SPAN, DT), jnp.float32), -5.0, 5.0)
    return (base * ramp * row_scale).astype(jnp.bfloat16)


def with_ends(values, rng, least, largest):
    dims = values.shape
    index_at = [jax.random.randint(jax.random.fold_in(rng, axis), (), 0, dims[axis]) for axis in range(len(dims))]
    values = values.at[tuple(index_at)].set(least)
    longest = dims.index(max(dims))
    index_at[longest] = (index_at[longest] + 1) % dims[longest]
    return values.at[tuple(index_at)].set(largest)


def steps_of(own_key, extent, cuts, least, top_value):
    level = 1.0
    for dim, blocks in cuts:
        draws = jax.random.uniform(jax.random.fold_in(jax.random.fold_in(own_key, 6), dim), (blocks,), jnp.float32, least / len(cuts), top_value / len(cuts))
        level = level * jnp.repeat(jnp.exp(draws), extent[dim] // blocks).reshape((-1,) + (1,) * (len(extent) - 1 - dim))
    return level


def centred(rng, shape, spread, reach, cuts=(), kind=jnp.bfloat16):
    array = jax.random.normal(rng, shape, jnp.float32) * spread
    if len(cuts) > 0:
        array = steps_of(rng, shape, cuts, -0.22, 0.18) * array
    return jnp.clip(array, min=-reach, max=reach).astype(kind)


def setup_inputs(seed: int = 0) -> dict:
    streams_of = jax.random.split(jax.random.key(seed), 7)
    teacher_rows = draw_teacher_rows(jax.random.fold_in(streams_of[6], 71), 0)
    projection = centred(streams_of[1], (DT, DS), DT ** -0.5, 0.0625, ((0, 8),))
    queries = draw_queries(jax.random.fold_in(streams_of[6], 71), 0)
    cache_kv = draw_cache_kv(jax.random.fold_in(streams_of[6], 71), 0)
    first_key = with_ends(jax.random.randint(streams_of[4], (REPL, SPAN // QBLOCK), 0, CACHE - SPAN + 1), jax.random.fold_in(streams_of[4], 1), 0, CACHE - SPAN).astype(jnp.int32)
    out_weight = centred(streams_of[5], (QH * HD, DS), (QH * HD) ** -0.5, 0.125)
    return dict(teacher_rows=teacher_rows, projection=projection, queries=queries, cache_kv=cache_kv, first_key=first_key, out_weight=out_weight)


norm_eps = 1e-05

def reference(teacher_rows, projection, queries, cache_kv, first_key, out_weight):
    rows32 = teacher_rows.astype(jnp.float32)
    mean_sq = lax.optimization_barrier(jnp.mean(rows32 * rows32, axis=-1, keepdims=True))
    normed = (rows32 * lax.rsqrt(mean_sq + norm_eps)).astype(jnp.bfloat16)
    shard_width = DT // N_TP
    target = jnp.zeros((REPL, SPAN, DS), jnp.float32)
    for shard_index in range(N_TP):
        slab_rows = normed[:, :, shard_index * shard_width:(shard_index + 1) * shard_width].reshape(REPL * SPAN, shard_width)
        partial_term = jnp.dot(slab_rows, projection[shard_index * shard_width:(shard_index + 1) * shard_width], preferred_element_type=jnp.float32)
        rounded = lax.optimization_barrier(partial_term.astype(jnp.bfloat16))
        target = target + rounded.astype(jnp.float32).reshape(REPL, SPAN, DS)
    group_size = QH // KVH
    score_scale = HD ** (-0.5)
    positions = CACHE - SPAN + jnp.arange(SPAN)
    key_positions = jnp.arange(CACHE)

    def one_replica(packed):
        query_rows, cache_rows, first_rows, target_rows = packed
        lower_bound = jnp.repeat(first_rows, QBLOCK, total_repeat_length=SPAN)
        visible = (key_positions[None, :] <= positions[:, None]) & (key_positions[None, :] >= lower_bound[:, None])
        keys32 = cache_rows[:, 0].astype(jnp.float32).reshape(CACHE, KVH, HD).transpose(1, 0, 2)
        values32 = cache_rows[:, 1].astype(jnp.float32).reshape(CACHE, KVH, HD).transpose(1, 0, 2)
        query32 = query_rows.astype(jnp.float32).reshape(SPAN, KVH, group_size, HD).transpose(1, 2, 0, 3)

        def scores_of(query_group, key_group):
            raw = jnp.einsum('gtd,sd->gts', query_group, key_group, precision=lax.Precision.HIGHEST) * score_scale
            return jnp.where(visible[None], raw, -jnp.inf)

        def forward(group_pack):
            query_group, key_group, value_group = group_pack
            scores = scores_of(query_group, key_group)
            row_max = lax.optimization_barrier(jnp.max(scores, axis=-1))
            probs = jnp.where(visible[None], jnp.exp(scores - row_max[..., None]), 0.0)
            row_total = lax.optimization_barrier(jnp.sum(probs, axis=-1))
            probs_low = lax.optimization_barrier(probs.astype(jnp.bfloat16)).astype(jnp.float32)
            summed = jnp.einsum('gts,sd->gtd', probs_low, value_group, precision=lax.Precision.HIGHEST)
            attended_group = summed / row_total[..., None]
            return (attended_group, row_max, row_total)
        attended, row_maxes, row_totals = lax.map(forward, (query32, keys32, values32))
        attended_rows = attended.transpose(2, 0, 1, 3).reshape(SPAN, QH * HD)
        hidden = jnp.dot(attended_rows.astype(jnp.bfloat16), out_weight, preferred_element_type=jnp.float32)
        inv_rms = lax.rsqrt(lax.optimization_barrier(jnp.mean(hidden * hidden, axis=-1, keepdims=True)) + norm_eps)
        scaled = hidden * inv_rms
        error = scaled - target_rows
        grad_hidden = inv_rms * (error - scaled * lax.optimization_barrier(jnp.mean(error * scaled, axis=-1, keepdims=True)))
        grad_attended = jnp.dot(grad_hidden.astype(jnp.bfloat16), out_weight.T, preferred_element_type=jnp.float32).astype(jnp.bfloat16)
        grad_heads = grad_attended.astype(jnp.float32).reshape(SPAN, KVH, group_size, HD).transpose(1, 2, 0, 3)
        deltas = lax.optimization_barrier(jnp.sum(grad_heads * attended, axis=-1))

        def backward(group_pack):
            query_group, key_group, value_group, grad_group, row_max, row_total, delta_group = group_pack
            scores = scores_of(query_group, key_group)
            weights = jnp.where(visible[None], jnp.exp(scores - row_max[..., None]), 0.0) / row_total[..., None]
            grad_weights = jnp.einsum('gtd,sd->gts', grad_group, value_group, precision=lax.Precision.HIGHEST)
            grad_scores = lax.optimization_barrier((weights * (grad_weights - delta_group[..., None])).astype(jnp.bfloat16))
            return jnp.einsum('gts,sd->gtd', grad_scores.astype(jnp.float32), key_group, precision=lax.Precision.HIGHEST) * score_scale
        grad_groups = lax.map(backward, (query32, keys32, values32, grad_heads, row_maxes, row_totals, deltas))
        grad_rows = grad_groups.transpose(2, 0, 1, 3).reshape(SPAN, QH * HD)
        return (scaled.astype(jnp.bfloat16), grad_rows)
    predicted, grad_queries = lax.map(one_replica, (queries, cache_kv, first_key, target))
    return (predicted, grad_queries)
```

```python
import functools
import math

import jax
import jax.numpy as jnp
from jax import lax
from jax.experimental import pallas as pl
from jax.experimental.pallas import tpu as pltpu
from jax.sharding import PartitionSpec as P

DT = 8192
QH = 16
KVH = 4
RING = 4
HD = 128
GROUP = QH // KVH
NORM_EPS = 1e-05
MASKED = -1e30
LOWEST = -1e29
SCALE = HD ** (-0.5)
SCALE2 = SCALE * math.log2(math.e)
bf16 = jnp.bfloat16
f32 = jnp.float32


def whole(memory_space=pltpu.VMEM):
    return pl.BlockSpec(memory_space=memory_space)


def params(mebibytes):
    return pltpu.CompilerParams(vmem_limit_bytes=mebibytes * 2**20)


def nt_dot(a, b):
    return lax.dot_general(a, b, (((1,), (1,)), ((), ())), preferred_element_type=f32)


def tn_dot(a, b):
    return lax.dot_general(a, b, (((0,), (0,)), ((), ())), preferred_element_type=f32)


def project_kernel(hops, cuts, _, rows_hbm, weight_hbm, *refs):
    outs, (rows_ref, weight_ref, row_sem, weight_sem) = refs[: len(cuts)], refs[len(cuts) :]
    tokens, width = rows_hbm.shape[1], weight_hbm.shape[1]
    strip = 512
    me = lax.axis_index("tp")
    base = me // RING * RING
    loads = []
    for i, hop in enumerate(hops):
        for z in range(2):
            replica = (base + z * RING) % (2 * RING) + (me + hop) % RING
            k = 2 * i + z
            loads.append(
                pltpu.make_async_copy(
                    rows_hbm.at[replica], rows_ref.at[pl.ds(k * tokens, tokens)], row_sem.at[k]
                )
            )
    strips = [
        pltpu.make_async_copy(
            weight_hbm.at[:, pl.ds(at, strip)], weight_ref.at[:, pl.ds(at, strip)], weight_sem.at[i]
        )
        for i, at in enumerate(range(0, width, strip))
    ]
    for copy in loads + strips:
        copy.start()
    for copy in loads:
        copy.wait()

    def put(block, at):
        size = block.shape[1]
        for out, (replica, count, first, end) in zip(outs, cuts):
            if first <= at < end:
                for z in range(count):
                    row = (replica + z) * tokens
                    out[z, :, at - first : at - first + size] = block[row : row + tokens]

    rows = rows_ref[...]
    for copy, at in zip(strips, range(0, width, strip)):
        copy.wait()
        put(
            jnp.dot(rows, weight_ref[:, at : at + strip], preferred_element_type=f32).astype(bf16),
            at,
        )
    rows32 = rows.astype(f32)
    squares = jnp.sum(rows32 * rows32, axis=-1, keepdims=True)
    high = squares.astype(bf16).astype(f32)
    lane = lax.broadcasted_iota(jnp.int32, (rows.shape[0], 128), 1)
    put(
        jnp.where(lane == me, high, jnp.where(lane == me + 8, squares - high, 0.0)).astype(bf16),
        width,
    )


def project(after, rows, weight, hops, cuts):
    _, tokens, depth = rows.shape
    width = weight.shape[1]
    count = 2 * len(hops)
    return pl.pallas_call(
        functools.partial(project_kernel, hops, cuts),
        in_specs=[whole(pl.ANY)] + [whole(pltpu.HBM)] * 2,
        out_specs=[whole()] * len(cuts),
        out_shape=[
            jax.ShapeDtypeStruct((z, tokens, end - first), bf16) for _, z, first, end in cuts
        ],
        scratch_shapes=[
            pltpu.VMEM((count * tokens, depth), bf16),
            pltpu.VMEM((depth, width), bf16),
            pltpu.SemaphoreType.DMA((count,)),
            pltpu.SemaphoreType.DMA((width // 512,)),
        ],
        compiler_params=params(16),
        cost_estimate=pl.CostEstimate(
            flops=4 * count * tokens * depth * width, bytes_accessed=8 * 2**20, transcendentals=0
        ),
        name="project",
    )(after, rows, weight)


def join_kernel(far_ref, below_ref, above_ref, up_ref, down_ref, all_ref):
    keys = far_ref.shape[0]
    half = keys // 2
    up_ref[:keys] = far_ref[...]
    up_ref[keys:] = below_ref[:half]
    down_ref[:keys] = far_ref[...]
    down_ref[keys:] = above_ref[half:]
    all_ref[:keys] = far_ref[...]
    all_ref[keys : 2 * keys] = below_ref[...]
    all_ref[2 * keys :] = above_ref[...]


def join(far, below, above):
    keys, width = far.shape
    rows = (keys + keys // 2, keys + keys // 2, 3 * keys)
    return pl.pallas_call(
        join_kernel,
        in_specs=[whole()] * 3,
        out_specs=[whole()] * 3,
        out_shape=[jax.ShapeDtypeStruct((r, width), bf16) for r in rows],
        compiler_params=params(16),
        name="join",
    )(far, below, above)


def add_kernel(up_in, down_in, *refs):
    ins, outs = refs[:4], refs[4:]
    cut = up_in.shape[-1]
    for z in range(2):
        up, down, up_out, down_out = ins[2 * z], ins[2 * z + 1], outs[2 * z], outs[2 * z + 1]
        up_out[0, :, :cut] = (up[0, :, :cut].astype(f32) + up_in[z].astype(f32)).astype(bf16)
        up_out[0, :, cut:] = up[0, :, cut:]
        down_out[0, :, :cut] = down[0, :, :cut]
        down_out[0, :, cut:] = (down[0, :, cut:].astype(f32) + down_in[z].astype(f32)).astype(bf16)


def add(up_in, down_in, *sums):
    return pl.pallas_call(
        add_kernel,
        in_specs=[whole()] * 6,
        out_specs=[whole()] * 4,
        out_shape=[jax.ShapeDtypeStruct(a.shape, bf16) for a in sums],
        compiler_params=params(16),
        name="add",
    )(up_in, down_in, *sums)


def query_group(q_ref, g):
    return jnp.concatenate(
        [q_ref[:, (GROUP * g + h) * HD : (GROUP * g + h + 1) * HD] for h in range(GROUP)], axis=0
    )


def fill_bias(first_ref, segments, n, shard_keys, bias_ref):
    tokens = bias_ref.shape[1]
    first_key, me = first_ref[0, 0], lax.axis_index("seq")
    first_token = (shard_keys - tokens) * n + me * tokens
    row = 0
    for flip, hop, core, first, rows in segments:
        shard = lax.rem((me ^ flip) + hop, n) ^ core
        key_at = shard * shard_keys + first + lax.broadcasted_iota(jnp.int32, (rows, tokens), 0)
        token_at = first_token + lax.broadcasted_iota(jnp.int32, (rows, tokens), 1)
        bias_ref[row : row + rows, :] = jnp.where(
            (key_at >= first_key) & (key_at <= token_at), 0.0, MASKED
        )
        row += rows


def blocks_of(arrays):
    found, row = [], 0
    for a in arrays:
        rows = a.shape[0]
        step = 256 if rows % 256 == 0 else rows
        for at in range(0, rows, step):
            found.append((a, at, row + at, step))
        row += rows
    return found


def spans_of(arrays):
    found, row = [], 0
    for a in arrays:
        found.append((a, row, a.shape[0]))
        row += a.shape[0]
    return found


def softmax_step(g, q_ref, kv_refs, bias_ref, probs_ref, top, total, acc):
    query = query_group(q_ref, g)

    def score(kv_ref, at, row, rows):
        bias = bias_ref[row : row + rows, :]
        return nt_dot(kv_ref[at : at + rows, g * HD : (g + 1) * HD], query) + jnp.concatenate(
            [bias] * GROUP, axis=1
        )

    new_top = top
    for block in blocks_of(kv_refs):
        new_top = jnp.maximum(new_top, jnp.max(score(*block), axis=0, keepdims=True))
    shift = new_top * SCALE2
    rescale = jnp.exp2(top * SCALE2 - shift)
    total = total * rescale
    acc = acc * rescale
    for block in blocks_of(kv_refs):
        probs = jnp.exp2(score(*block) * SCALE2 - shift)
        total = total + jnp.sum(probs, axis=0, keepdims=True)
        probs_ref[g, block[2] : block[2] + block[3], :] = probs.astype(bf16)
    for kv_ref, row, rows in spans_of(kv_refs):
        acc = acc + tn_dot(
            kv_ref[:, (KVH + g) * HD : (KVH + g + 1) * HD], probs_ref[g, row : row + rows, :]
        )
    return new_top, total, acc


def forward_kernel(segments, n, shard_keys, n_arrays, with_state, *refs):
    first_ref, q_ref = refs[:2]
    kv_refs, refs = refs[3 : 3 + n_arrays], refs[3 + n_arrays :]
    if with_state:
        m_in, l_in, acc_in = refs[:3]
        refs = refs[3:]
    probs_ref, m_out, l_out, acc_out, bias_ref = refs
    span = GROUP * q_ref.shape[0]
    fill_bias(first_ref, segments, n, shard_keys, bias_ref)
    for g in range(KVH):
        cols = slice(g * span, (g + 1) * span)
        if with_state:
            state = m_in[:, cols], l_in[:, cols], acc_in[g]
        else:
            state = (
                jnp.full((1, span), LOWEST, f32),
                jnp.zeros((1, span), f32),
                jnp.zeros((HD, span), f32),
            )
        m_out[:, cols], l_out[:, cols], acc_out[g] = softmax_step(
            g, q_ref, kv_refs, bias_ref, probs_ref, *state
        )


def forward(first_key, q, after, arrays, segments, n, shard_keys, state):
    keys = sum(a.shape[0] for a in arrays)
    tokens = q.shape[0]
    wide = QH * tokens
    span = GROUP * tokens
    state = tuple(state) if state is not None else ()
    return pl.pallas_call(
        functools.partial(
            forward_kernel, tuple(segments), n, shard_keys, len(arrays), bool(state)
        ),
        in_specs=[whole(pltpu.SMEM), whole(), whole(pl.ANY)]
        + [whole()] * (len(arrays) + len(state)),
        out_specs=[whole()] * 4,
        out_shape=[
            jax.ShapeDtypeStruct((KVH, keys, span), bf16),
            jax.ShapeDtypeStruct((1, wide), f32),
            jax.ShapeDtypeStruct((1, wide), f32),
            jax.ShapeDtypeStruct((KVH, HD, span), f32),
        ],
        scratch_shapes=[pltpu.VMEM((keys, tokens), f32)],
        compiler_params=params(14),
        cost_estimate=pl.CostEstimate(
            flops=12 * keys * wide * HD, bytes_accessed=keys * wide * 2, transcendentals=keys * wide
        ),
        name="forward",
    )(first_key, q, after, *arrays, *state)


def hidden_kernel(count, segments, n, shard_keys, *refs):
    first_ref, q_ref, m_in, l_in, acc_in, weight_hbm = refs[:6]
    arrays, refs = refs[6 : 6 + count], refs[6 + count :]
    weight_ref, hidden_ref, kv_ref, probs_ref, m_ref, l_ref, turned_ref, bias_ref, sem = refs
    tokens = q_ref.shape[0]
    span = GROUP * tokens
    load = pltpu.make_async_copy(weight_hbm, weight_ref, sem.at[0])
    load.start()
    for a, row, rows in spans_of(arrays):
        kv_ref[row : row + rows] = a[...]
    fill_bias(first_ref, segments, n, shard_keys, bias_ref)
    rows = []
    for g in range(KVH):
        cols = slice(g * span, (g + 1) * span)
        top, total, acc = softmax_step(
            g, q_ref, [kv_ref], bias_ref, probs_ref, m_in[:, cols], l_in[:, cols], acc_in[g]
        )
        m_ref[:, cols] = top
        l_ref[:, cols] = total
        acc = acc / total
        turned_ref[g] = acc
        rows += [acc[:, h * tokens : (h + 1) * tokens].T.astype(bf16) for h in range(GROUP)]
    load.wait()
    hidden_ref[...] = jnp.dot(
        jnp.concatenate(rows, axis=1), weight_ref[...], preferred_element_type=f32
    )


def project_out(first_key, q, state, weight, arrays, segments, n, shard_keys):
    keys = sum(a.shape[0] for a in arrays)
    tokens = q.shape[0]
    wide = QH * tokens
    span = GROUP * tokens
    width = weight.shape[1]
    return pl.pallas_call(
        functools.partial(hidden_kernel, len(arrays), tuple(segments), n, shard_keys),
        in_specs=[whole(pltpu.SMEM)]
        + [whole()] * 4
        + [whole(pltpu.HBM)]
        + [whole()] * len(arrays),
        out_specs=[whole()] * 7,
        out_shape=[
            jax.ShapeDtypeStruct(weight.shape, bf16),
            jax.ShapeDtypeStruct((tokens, width), f32),
            jax.ShapeDtypeStruct((keys, arrays[0].shape[1]), bf16),
            jax.ShapeDtypeStruct((KVH, keys, span), bf16),
            jax.ShapeDtypeStruct((1, wide), f32),
            jax.ShapeDtypeStruct((1, wide), f32),
            jax.ShapeDtypeStruct((KVH, HD, span), f32),
        ],
        scratch_shapes=[pltpu.VMEM((keys, tokens), f32), pltpu.SemaphoreType.DMA((1,))],
        compiler_params=params(14),
        cost_estimate=pl.CostEstimate(
            flops=1000, bytes_accessed=1000, transcendentals=0
        ),
        name="project_out",
    )(first_key, q, *state, weight, *arrays)


def tail_kernel(counts, *refs):
    calls = len(counts)
    weight_ref, hidden_ref, l_ref, attended_ref = refs[:4]
    target_refs, refs = refs[4:8], refs[8:]
    groups = []
    for count in counts:
        groups.append(refs[:count])
        refs = refs[count:]
    tops_refs, probs_refs, refs = refs[:calls], refs[calls : 2 * calls], refs[2 * calls :]
    predicted_ref, out_ref, grad_ref, delta_ref, turned_ref = refs
    m_ref = tops_refs[0]
    tokens = predicted_ref.shape[0]
    width = weight_ref.shape[1]
    span = GROUP * tokens
    hidden = hidden_ref[...]
    inv_rms = lax.rsqrt(jnp.mean(hidden * hidden, axis=-1, keepdims=True) + NORM_EPS)
    scaled = hidden * inv_rms
    predicted_ref[...] = scaled.astype(bf16)
    target = sum(t[0].astype(f32) for t in target_refs)
    squares = jnp.sum(target[:, width:], axis=-1, keepdims=True)
    target = target[:, :width] * lax.rsqrt(squares / DT + NORM_EPS)
    error = scaled - target
    grad = inv_rms * (error - scaled * jnp.mean(error * scaled, axis=-1, keepdims=True))
    grad_turned = nt_dot(weight_ref[...], grad.astype(bf16)).astype(bf16)
    grad_ref[...] = grad_turned
    for head in range(QH):
        g, h = divmod(head, GROUP)
        block = (
            grad_turned[head * HD : (head + 1) * HD].astype(f32)
            * attended_ref[g, :, h * tokens : (h + 1) * tokens]
        )
        delta_ref[:, head * tokens : (head + 1) * tokens] = jnp.sum(block, axis=0, keepdims=True)
    for c, (kv_refs, weights_ref, tops_ref) in enumerate(zip(groups, probs_refs, tops_refs)):
        for g in range(KVH):
            cols = slice(g * span, (g + 1) * span)
            grad_g = jnp.concatenate(
                [
                    grad_ref[(GROUP * g + h) * HD : (GROUP * g + h + 1) * HD, :]
                    for h in range(GROUP)
                ],
                axis=1,
            )
            delta = delta_ref[:, cols]
            part = None
            for keys_ref, row, rows in spans_of(kv_refs):
                slope = jnp.dot(
                    keys_ref[:, (KVH + g) * HD : (KVH + g + 1) * HD],
                    grad_g,
                    preferred_element_type=f32,
                )
                probs = weights_ref[g, row : row + rows, :].astype(f32)
                low = (probs * (slope - delta)).astype(bf16)
                term = tn_dot(keys_ref[:, g * HD : (g + 1) * HD], low)
                part = term if part is None else part + term
            factor = SCALE / l_ref[:, cols]
            if c > 0:
                factor = factor * jnp.exp2((tops_ref[:, cols] - m_ref[:, cols]) * SCALE2)
            part = part * factor
            if c > 0:
                part = part + turned_ref[g]
            if c + 1 < calls:
                turned_ref[g] = part
                continue
            for h in range(GROUP):
                head = GROUP * g + h
                out_ref[:, head * HD : (head + 1) * HD] = part[
                    :, h * tokens : (h + 1) * tokens
                ].T


def tail(weight, hidden, l, attended, targets, groups, tops, probs):
    arrays = [a for g in groups for a in g]
    keys = sum(a.shape[0] for a in arrays)
    tokens, width = hidden.shape
    wide = QH * tokens
    return pl.pallas_call(
        functools.partial(tail_kernel, tuple(len(g) for g in groups)),
        in_specs=[whole()] * (4 + len(targets) + len(arrays) + 2 * len(groups)),
        out_specs=[whole()] * 2,
        out_shape=[
            jax.ShapeDtypeStruct((tokens, width), bf16),
            jax.ShapeDtypeStruct((tokens, QH * HD), f32),
        ],
        scratch_shapes=[
            pltpu.VMEM((QH * HD, tokens), bf16),
            pltpu.VMEM((1, wide), f32),
            pltpu.VMEM((KVH, HD, GROUP * tokens), f32),
        ],
        compiler_params=params(12),
        cost_estimate=pl.CostEstimate(
            flops=8 * keys * wide * HD, bytes_accessed=keys * wide * 2, transcendentals=0
        ),
        name="tail",
    )(weight, hidden, l, attended, *targets, *arrays, *tops, *probs)


def shards(teacher_rows, projection, queries, cache_kv, first_key, out_weight):
    n = lax.axis_size("seq")
    parts = lax.axis_size("tp")
    keys = cache_kv.shape[1]
    half = keys // 2
    width = projection.shape[1]
    wide = width + 128
    cut = width // 2
    together = lax.optimization_barrier

    def send(x, flip, hop=0):
        return lax.ppermute(x, "seq", [(i, ((i ^ flip) + hop) % n) for i in range(n)])

    def send_tp(x, flip, hop=0):
        perm = [(i, (i ^ flip) // RING * RING + (i + hop) % RING) for i in range(parts)]
        return lax.ppermute(x, "tp", perm)

    def pair(x, swapped, runs):
        here = [(flip, hop % n, 0, first, rows) for flip, hop, first, rows in runs]
        there = [(flip, hop % n, 1, first, rows) for flip, hop, first, rows in runs]
        return [(x, here), (swapped, there)]

    def split(call):
        return [a for a, _ in call], [s for _, runs in call for s in runs]

    q = queries[0]
    teacher_rows, projection, out_weight = (
        pltpu.with_memory_space_constraint(a, pltpu.HBM)
        for a in (teacher_rows, projection, out_weight)
    )
    own = cache_kv.reshape(keys, -1)
    far = send(own, 2)
    below = send(own, 0, 4)
    above = send(own, 0, -4)
    own_s = send(own, 1)
    x_up, x_down = project(own_s, teacher_rows, projection, (2,), ((0, 2, 0, cut), (0, 2, cut, wide)))
    x_up_in = send_tp(x_up, 0, 1)
    x_down_in = send_tp(x_down, 0, -1)
    sums = project(x_up, teacher_rows, projection, (1, -1, 0), tuple((i, 1, 0, wide) for i in range(6)))
    far, below, above, sums = together((far, below, above, tuple(sums)))
    up_mine, up_theirs, down_mine, down_theirs, own_mine, own_theirs = sums
    up_two, down_two, three = join(far, below, above)
    y_up = send(up_two, 0, 4)
    y_down = send(down_two, 0, -4)
    x_up_in, x_down_in, three = together((x_up_in, x_down_in, three))
    three_s = send(three, 1)
    up_mine, down_mine, up_theirs, down_theirs = add(
        x_up_in, x_down_in, up_mine, down_mine, up_theirs, down_theirs
    )
    up_theirs_in = send_tp(up_theirs, 0, 1)
    down_theirs_in = send_tp(down_theirs, 0, -1)
    first, segments = split(
        pair(own, own_s, [(0, 0, 0, keys)])
        + pair(three, three_s, [(2, 0, 0, keys), (0, -4, 0, keys), (0, 4, 0, keys)])
    )
    first_probs, *state = forward(first_key, q, up_theirs, first, segments, n, keys, None)
    first_tops = state[0]
    y_up, y_down, up_theirs_in, down_theirs_in, up_mine, down_mine, state = together(
        (y_up, y_down, up_theirs_in, down_theirs_in, up_mine, down_mine, tuple(state))
    )
    y_up_s, y_down_s = send(y_up, 1), send(y_down, 1)
    theirs = up_theirs_in.astype(f32) + down_theirs_in.astype(f32) + own_theirs.astype(f32)
    theirs = theirs.astype(bf16)
    cross = send_tp(theirs, RING)
    last_up = send(y_up[:half], 0, 4)
    last_down = send(y_down[half:keys], 0, -4)
    up_mine_in = send_tp(up_mine, 0, 1)
    down_mine_in = send_tp(down_mine, 0, -1)
    second, segments = split(
        pair(y_up, y_up_s, [(2, -4, 0, keys), (0, -8, 0, half)])
        + pair(y_down, y_down_s, [(2, 4, 0, keys), (0, 8, half, half)])
    )
    second_probs, *state = forward(first_key, q, theirs, second, segments, n, keys, state)
    second_tops = state[0]
    last_up, last_down, state = together((last_up, last_down, tuple(state)))
    last = jnp.concatenate([last_up, last_down])
    last, segments = split(
        pair(last, send(last, 1), [(2, -8, 0, half), (2, 8, half, half)])
    )
    weight, hidden, last_kv, last_probs, top, total, attended = project_out(
        first_key, q, state, out_weight, last, segments, n, keys
    )
    predicted, grad_queries = tail(
        weight,
        hidden,
        total,
        attended,
        [up_mine_in, down_mine_in, own_mine, cross],
        [[last_kv], first, second],
        [top, first_tops, second_tops],
        [last_probs, first_probs, second_probs],
    )
    return predicted[None], grad_queries[None]


def solution(mesh):
    placed = (
        P(None, "seq", "tp"),
        P("tp", None),
        P("tp", "seq", None),
        P("tp", "seq", None, None),
        P("tp", "seq"),
        P(),
    )
    return jax.shard_map(
        shards,
        mesh=mesh,
        in_specs=placed,
        out_specs=(P("tp", "seq", None), P("tp", "seq", None)),
        check_vma=False,
    )
```

```python
import functools
import math

import jax
import jax.numpy as jnp
from jax import lax
from jax.experimental import pallas as pl
from jax.experimental.pallas import tpu as pltpu
from jax.sharding import PartitionSpec as P

DT = 8192
QH = 16
KVH = 4
RING = 4
HD = 128
GROUP = QH // KVH
NORM_EPS = 1e-05
MASKED = -1e30
LOWEST = -1e29
SCALE = HD ** (-0.5)
SCALE2 = SCALE * math.log2(math.e)
bf16 = jnp.bfloat16
f32 = jnp.float32


def whole(memory_space=pltpu.VMEM):
    return pl.BlockSpec(memory_space=memory_space)


def params(mebibytes):
    return pltpu.CompilerParams(vmem_limit_bytes=mebibytes * 2**20)


def nt_dot(a, b):
    return lax.dot_general(a, b, (((1,), (1,)), ((), ())), preferred_element_type=f32)


def tn_dot(a, b):
    return lax.dot_general(a, b, (((0,), (0,)), ((), ())), preferred_element_type=f32)


def project_kernel(hops, cuts, _, rows_hbm, weight_hbm, *refs):
    outs, (rows_ref, weight_ref, row_sem, weight_sem) = refs[: len(cuts)], refs[len(cuts) :]
    tokens, width = rows_hbm.shape[1], weight_hbm.shape[1]
    strip = 512
    me = lax.axis_index("tp")
    base = me // RING * RING
    loads = []
    for i, hop in enumerate(hops):
        for z in range(2):
            replica = (base + z * RING) % (2 * RING) + (me + hop) % RING
            k = 2 * i + z
            loads.append(
                pltpu.make_async_copy(
                    rows_hbm.at[replica], rows_ref.at[pl.ds(k * tokens, tokens)], row_sem.at[k]
                )
            )
    strips = [
        pltpu.make_async_copy(
            weight_hbm.at[:, pl.ds(at, strip)], weight_ref.at[:, pl.ds(at, strip)], weight_sem.at[i]
        )
        for i, at in enumerate(range(0, width, strip))
    ]
    for copy in loads + strips:
        copy.start()
    for copy in loads:
        copy.wait()

    def put(block, at):
        size = block.shape[1]
        for out, (replica, count, first, end) in zip(outs, cuts):
            if first <= at < end:
                for z in range(count):
                    row = (replica + z) * tokens
                    out[z, :, at - first : at - first + size] = block[row : row + tokens]

    rows = rows_ref[...]
    for copy, at in zip(strips, range(0, width, strip)):
        copy.wait()
        put(
            jnp.dot(rows, weight_ref[:, at : at + strip], preferred_element_type=f32).astype(bf16),
            at,
        )
    rows32 = rows.astype(f32)
    squares = jnp.sum(rows32 * rows32, axis=-1, keepdims=True)
    high = squares.astype(bf16).astype(f32)
    lane = lax.broadcasted_iota(jnp.int32, (rows.shape[0], 128), 1)
    put(
        jnp.where(lane == me, high, jnp.where(lane == me + 8, squares - high, 0.0)).astype(bf16),
        width,
    )


def project(after, rows, weight, hops, cuts):
    _, tokens, depth = rows.shape
    width = weight.shape[1]
    count = 2 * len(hops)
    return pl.pallas_call(
        functools.partial(project_kernel, hops, cuts),
        in_specs=[whole(pl.ANY)] + [whole(pltpu.HBM)] * 2,
        out_specs=[whole()] * len(cuts),
        out_shape=[
            jax.ShapeDtypeStruct((z, tokens, end - first), bf16) for _, z, first, end in cuts
        ],
        scratch_shapes=[
            pltpu.VMEM((count * tokens, depth), bf16),
            pltpu.VMEM((depth, width), bf16),
            pltpu.SemaphoreType.DMA((count,)),
            pltpu.SemaphoreType.DMA((width // 512,)),
        ],
        compiler_params=params(16),
        cost_estimate=pl.CostEstimate(
            flops=4 * count * tokens * depth * width, bytes_accessed=8 * 2**20, transcendentals=0
        ),
        name="project",
    )(after, rows, weight)


def join_kernel(far_ref, below_ref, above_ref, up_ref, down_ref, both_ref):
    keys = far_ref.shape[0]
    half = keys // 2
    up_ref[:keys] = far_ref[...]
    up_ref[keys:] = below_ref[:half]
    down_ref[:keys] = far_ref[...]
    down_ref[keys:] = above_ref[half:]
    both_ref[:keys] = below_ref[...]
    both_ref[keys:] = above_ref[...]


def join(far, below, above):
    keys, width = far.shape
    rows = (keys + keys // 2, keys + keys // 2, 2 * keys)
    return pl.pallas_call(
        join_kernel,
        in_specs=[whole()] * 3,
        out_specs=[whole()] * 3,
        out_shape=[jax.ShapeDtypeStruct((r, width), bf16) for r in rows],
        compiler_params=params(16),
        name="join",
    )(far, below, above)


def add_kernel(up_in, down_in, *refs):
    ins, outs = refs[:4], refs[4:]
    cut = up_in.shape[-1]
    for z in range(2):
        up, down, up_out, down_out = ins[2 * z], ins[2 * z + 1], outs[2 * z], outs[2 * z + 1]
        up_out[0, :, :cut] = (up[0, :, :cut].astype(f32) + up_in[z].astype(f32)).astype(bf16)
        up_out[0, :, cut:] = up[0, :, cut:]
        down_out[0, :, :cut] = down[0, :, :cut]
        down_out[0, :, cut:] = (down[0, :, cut:].astype(f32) + down_in[z].astype(f32)).astype(bf16)


def add(up_in, down_in, *sums):
    return pl.pallas_call(
        add_kernel,
        in_specs=[whole()] * 6,
        out_specs=[whole()] * 4,
        out_shape=[jax.ShapeDtypeStruct(a.shape, bf16) for a in sums],
        compiler_params=params(16),
        name="add",
    )(up_in, down_in, *sums)


def query_group(q_ref, g):
    return jnp.concatenate(
        [q_ref[:, (GROUP * g + h) * HD : (GROUP * g + h + 1) * HD] for h in range(GROUP)], axis=0
    )


def fill_bias(first_ref, segments, n, shard_keys, bias_ref):
    tokens = bias_ref.shape[1]
    first_key, me = first_ref[0, 0], lax.axis_index("seq")
    first_token = (shard_keys - tokens) * n + me * tokens
    row = 0
    for flip, hop, core, first, rows in segments:
        shard = lax.rem((me ^ flip) + hop, n) ^ core
        key_at = shard * shard_keys + first + lax.broadcasted_iota(jnp.int32, (rows, tokens), 0)
        token_at = first_token + lax.broadcasted_iota(jnp.int32, (rows, tokens), 1)
        bias_ref[row : row + rows, :] = jnp.where(
            (key_at >= first_key) & (key_at <= token_at), 0.0, MASKED
        )
        row += rows


def blocks_of(arrays):
    found, row = [], 0
    for a in arrays:
        rows = a.shape[0]
        step = 256 if rows % 256 == 0 else rows
        for at in range(0, rows, step):
            found.append((a, at, row + at, step))
        row += rows
    return found


def spans_of(arrays):
    found, row = [], 0
    for a in arrays:
        found.append((a, row, a.shape[0]))
        row += a.shape[0]
    return found


def softmax_step(g, q_ref, kv_refs, bias_ref, probs_ref, top, total, acc):
    query = query_group(q_ref, g)

    def score(kv_ref, at, row, rows):
        bias = bias_ref[row : row + rows, :]
        return nt_dot(kv_ref[at : at + rows, g * HD : (g + 1) * HD], query) + jnp.concatenate(
            [bias] * GROUP, axis=1
        )

    new_top = top
    for block in blocks_of(kv_refs):
        new_top = jnp.maximum(new_top, jnp.max(score(*block), axis=0, keepdims=True))
    shift = new_top * SCALE2
    rescale = jnp.exp2(top * SCALE2 - shift)
    total = total * rescale
    acc = acc * rescale
    for block in blocks_of(kv_refs):
        probs = jnp.exp2(score(*block) * SCALE2 - shift)
        total = total + jnp.sum(probs, axis=0, keepdims=True)
        probs_ref[g, block[2] : block[2] + block[3], :] = probs.astype(bf16)
    for kv_ref, row, rows in spans_of(kv_refs):
        acc = acc + tn_dot(
            kv_ref[:, (KVH + g) * HD : (KVH + g + 1) * HD], probs_ref[g, row : row + rows, :]
        )
    return new_top, total, acc


def forward_kernel(segments, n, shard_keys, n_arrays, with_state, *refs):
    first_ref, q_ref = refs[:2]
    kv_refs, refs = refs[3 : 3 + n_arrays], refs[3 + n_arrays :]
    if with_state:
        m_in, l_in, acc_in = refs[:3]
        refs = refs[3:]
    probs_ref, m_out, l_out, acc_out, bias_ref = refs
    span = GROUP * q_ref.shape[0]
    fill_bias(first_ref, segments, n, shard_keys, bias_ref)
    for g in range(KVH):
        cols = slice(g * span, (g + 1) * span)
        if with_state:
            state = m_in[:, cols], l_in[:, cols], acc_in[g]
        else:
            state = (
                jnp.full((1, span), LOWEST, f32),
                jnp.zeros((1, span), f32),
                jnp.zeros((HD, span), f32),
            )
        m_out[:, cols], l_out[:, cols], acc_out[g] = softmax_step(
            g, q_ref, kv_refs, bias_ref, probs_ref, *state
        )


def forward(first_key, q, after, arrays, segments, n, shard_keys, state):
    keys = sum(a.shape[0] for a in arrays)
    tokens = q.shape[0]
    wide = QH * tokens
    span = GROUP * tokens
    state = tuple(state) if state is not None else ()
    return pl.pallas_call(
        functools.partial(
            forward_kernel, tuple(segments), n, shard_keys, len(arrays), bool(state)
        ),
        in_specs=[whole(pltpu.SMEM), whole(), whole(pl.ANY)]
        + [whole()] * (len(arrays) + len(state)),
        out_specs=[whole()] * 4,
        out_shape=[
            jax.ShapeDtypeStruct((KVH, keys, span), bf16),
            jax.ShapeDtypeStruct((1, wide), f32),
            jax.ShapeDtypeStruct((1, wide), f32),
            jax.ShapeDtypeStruct((KVH, HD, span), f32),
        ],
        scratch_shapes=[pltpu.VMEM((keys, tokens), f32)],
        compiler_params=params(14),
        cost_estimate=pl.CostEstimate(
            flops=1000, bytes_accessed=1000, transcendentals=0
        ),
        name="forward",
    )(first_key, q, after, *arrays, *state)


def hidden_kernel(count, segments, n, shard_keys, *refs):
    first_ref, q_ref, m_in, l_in, acc_in, weight_hbm = refs[:6]
    arrays, refs = refs[6 : 6 + count], refs[6 + count :]
    weight_ref, hidden_ref, kv_ref, probs_ref, m_ref, l_ref, turned_ref, bias_ref, sem = refs
    tokens = q_ref.shape[0]
    span = GROUP * tokens
    load = pltpu.make_async_copy(weight_hbm, weight_ref, sem.at[0])
    load.start()
    for a, row, rows in spans_of(arrays):
        kv_ref[row : row + rows] = a[...]
    fill_bias(first_ref, segments, n, shard_keys, bias_ref)
    rows = []
    for g in range(KVH):
        cols = slice(g * span, (g + 1) * span)
        top, total, acc = softmax_step(
            g, q_ref, [kv_ref], bias_ref, probs_ref, m_in[:, cols], l_in[:, cols], acc_in[g]
        )
        m_ref[:, cols] = top
        l_ref[:, cols] = total
        acc = acc / total
        turned_ref[g] = acc
        rows += [acc[:, h * tokens : (h + 1) * tokens].T.astype(bf16) for h in range(GROUP)]
    load.wait()
    hidden_ref[...] = jnp.dot(
        jnp.concatenate(rows, axis=1), weight_ref[...], preferred_element_type=f32
    )


def project_out(first_key, q, state, weight, arrays, segments, n, shard_keys):
    keys = sum(a.shape[0] for a in arrays)
    tokens = q.shape[0]
    wide = QH * tokens
    span = GROUP * tokens
    width = weight.shape[1]
    return pl.pallas_call(
        functools.partial(hidden_kernel, len(arrays), tuple(segments), n, shard_keys),
        in_specs=[whole(pltpu.SMEM)]
        + [whole()] * 4
        + [whole(pltpu.HBM)]
        + [whole()] * len(arrays),
        out_specs=[whole()] * 7,
        out_shape=[
            jax.ShapeDtypeStruct(weight.shape, bf16),
            jax.ShapeDtypeStruct((tokens, width), f32),
            jax.ShapeDtypeStruct((keys, arrays[0].shape[1]), bf16),
            jax.ShapeDtypeStruct((KVH, keys, span), bf16),
            jax.ShapeDtypeStruct((1, wide), f32),
            jax.ShapeDtypeStruct((1, wide), f32),
            jax.ShapeDtypeStruct((KVH, HD, span), f32),
        ],
        scratch_shapes=[pltpu.VMEM((keys, tokens), f32), pltpu.SemaphoreType.DMA((1,))],
        compiler_params=params(14),
        cost_estimate=pl.CostEstimate(
            flops=1000, bytes_accessed=1000, transcendentals=0
        ),
        name="project_out",
    )(first_key, q, *state, weight, *arrays)


def tail_kernel(counts, *refs):
    calls = len(counts)
    weight_ref, hidden_ref, l_ref, attended_ref = refs[:4]
    target_refs, refs = refs[4:8], refs[8:]
    groups = []
    for count in counts:
        groups.append(refs[:count])
        refs = refs[count:]
    tops_refs, probs_refs, refs = refs[:calls], refs[calls : 2 * calls], refs[2 * calls :]
    predicted_ref, out_ref, grad_ref, delta_ref, turned_ref = refs
    m_ref = tops_refs[0]
    tokens = predicted_ref.shape[0]
    width = weight_ref.shape[1]
    span = GROUP * tokens
    hidden = hidden_ref[...]
    inv_rms = lax.rsqrt(jnp.mean(hidden * hidden, axis=-1, keepdims=True) + NORM_EPS)
    scaled = hidden * inv_rms
    predicted_ref[...] = scaled.astype(bf16)
    target = sum(t[0].astype(f32) for t in target_refs)
    squares = jnp.sum(target[:, width:], axis=-1, keepdims=True)
    target = target[:, :width] * lax.rsqrt(squares / DT + NORM_EPS)
    error = scaled - target
    grad = inv_rms * (error - scaled * jnp.mean(error * scaled, axis=-1, keepdims=True))
    grad_turned = nt_dot(weight_ref[...], grad.astype(bf16)).astype(bf16)
    grad_ref[...] = grad_turned
    for head in range(QH):
        g, h = divmod(head, GROUP)
        block = (
            grad_turned[head * HD : (head + 1) * HD].astype(f32)
            * attended_ref[g, :, h * tokens : (h + 1) * tokens]
        )
        delta_ref[:, head * tokens : (head + 1) * tokens] = jnp.sum(block, axis=0, keepdims=True)
    for c, (kv_refs, weights_ref, tops_ref) in enumerate(zip(groups, probs_refs, tops_refs)):
        for g in range(KVH):
            cols = slice(g * span, (g + 1) * span)
            grad_g = jnp.concatenate(
                [
                    grad_ref[(GROUP * g + h) * HD : (GROUP * g + h + 1) * HD, :]
                    for h in range(GROUP)
                ],
                axis=1,
            )
            delta = delta_ref[:, cols]
            part = None
            for keys_ref, row, rows in spans_of(kv_refs):
                slope = jnp.dot(
                    keys_ref[:, (KVH + g) * HD : (KVH + g + 1) * HD],
                    grad_g,
                    preferred_element_type=f32,
                )
                probs = weights_ref[g, row : row + rows, :].astype(f32)
                low = (probs * (slope - delta)).astype(bf16)
                term = tn_dot(keys_ref[:, g * HD : (g + 1) * HD], low)
                part = term if part is None else part + term
            factor = SCALE / l_ref[:, cols]
            if c > 0:
                factor = factor * jnp.exp2((tops_ref[:, cols] - m_ref[:, cols]) * SCALE2)
            part = part * factor
            if c > 0:
                part = part + turned_ref[g]
            if c + 1 < calls:
                turned_ref[g] = part
                continue
            for h in range(GROUP):
                head = GROUP * g + h
                out_ref[:, head * HD : (head + 1) * HD] = part[
                    :, h * tokens : (h + 1) * tokens
                ].T


def tail(weight, hidden, l, attended, targets, groups, tops, probs):
    arrays = [a for g in groups for a in g]
    keys = sum(a.shape[0] for a in arrays)
    tokens, width = hidden.shape
    wide = QH * tokens
    return pl.pallas_call(
        functools.partial(tail_kernel, tuple(len(g) for g in groups)),
        in_specs=[whole()] * (4 + len(targets) + len(arrays) + 2 * len(groups)),
        out_specs=[whole()] * 2,
        out_shape=[
            jax.ShapeDtypeStruct((tokens, width), bf16),
            jax.ShapeDtypeStruct((tokens, QH * HD), f32),
        ],
        scratch_shapes=[
            pltpu.VMEM((QH * HD, tokens), bf16),
            pltpu.VMEM((1, wide), f32),
            pltpu.VMEM((KVH, HD, GROUP * tokens), f32),
        ],
        compiler_params=params(12),
        cost_estimate=pl.CostEstimate(
            flops=8 * keys * wide * HD, bytes_accessed=keys * wide * 2, transcendentals=0
        ),
        name="tail",
    )(weight, hidden, l, attended, *targets, *arrays, *tops, *probs)


def shards(teacher_rows, projection, queries, cache_kv, first_key, out_weight):
    n = lax.axis_size("seq")
    parts = lax.axis_size("tp")
    keys = cache_kv.shape[1]
    half = keys // 2
    width = projection.shape[1]
    wide = width + 128
    cut = width // 2
    together = lax.optimization_barrier

    def send(x, flip, hop=0):
        return lax.ppermute(x, "seq", [(i, ((i ^ flip) + hop) % n) for i in range(n)])

    def send_tp(x, flip, hop=0):
        perm = [(i, (i ^ flip) // RING * RING + (i + hop) % RING) for i in range(parts)]
        return lax.ppermute(x, "tp", perm)

    def pair(x, swapped, runs):
        here = [(flip, hop % n, 0, first, rows) for flip, hop, first, rows in runs]
        there = [(flip, hop % n, 1, first, rows) for flip, hop, first, rows in runs]
        return [(x, here), (swapped, there)]

    def split(call):
        return [a for a, _ in call], [s for _, runs in call for s in runs]

    q = queries[0]
    teacher_rows, projection, out_weight = (
        pltpu.with_memory_space_constraint(a, pltpu.HBM)
        for a in (teacher_rows, projection, out_weight)
    )
    own = cache_kv.reshape(keys, -1)
    far = send(own, 2)
    below = send(own, 0, 4)
    above = send(own, 0, -4)
    own_s = send(own, 1)
    x_up, x_down = project(own_s, teacher_rows, projection, (2,), ((0, 2, 0, cut), (0, 2, cut, wide)))
    x_up_in = send_tp(x_up, 0, 1)
    x_down_in = send_tp(x_down, 0, -1)
    sums = project(x_up, teacher_rows, projection, (1, -1, 0), tuple((i, 1, 0, wide) for i in range(6)))
    far, below, above, sums = together((far, below, above, tuple(sums)))
    up_mine, up_theirs, down_mine, down_theirs, own_mine, own_theirs = sums
    up_two, down_two, near = join(far, below, above)
    y_up = send(up_two, 0, 4)
    y_down = send(down_two, 0, -4)
    near_s = send(near, 1)
    x_up_in, x_down_in, up_two = together((x_up_in, x_down_in, up_two))
    up_mine, down_mine, up_theirs, down_theirs = add(
        x_up_in, x_down_in, up_mine, down_mine, up_theirs, down_theirs
    )
    up_theirs_in = send_tp(up_theirs, 0, 1)
    down_theirs_in = send_tp(down_theirs, 0, -1)
    first, segments = split(
        pair(own, own_s, [(0, 0, 0, keys)])
        + [(far, [(2, 0, 0, 0, keys)])]
        + pair(near, near_s, [(0, -4, 0, keys), (0, 4, 0, keys)])
    )
    first_probs, *state = forward(first_key, q, up_theirs, first, segments, n, keys, None)
    first_tops = state[0]
    y_up, y_down, up_theirs_in, down_theirs_in, up_mine, down_mine, state = together(
        (y_up, y_down, up_theirs_in, down_theirs_in, up_mine, down_mine, tuple(state))
    )
    y_up_s, y_down_s = send(y_up, 1), send(y_down, 1)
    theirs = up_theirs_in.astype(f32) + down_theirs_in.astype(f32) + own_theirs.astype(f32)
    theirs = theirs.astype(bf16)
    cross = send_tp(theirs, RING)
    last_up = send(y_up[:half], 0, 4)
    last_down = send(y_down[half:keys], 0, -4)
    up_mine_in = send_tp(up_mine, 0, 1)
    down_mine_in = send_tp(down_mine, 0, -1)
    far, state = together((far, tuple(state)))
    far_s = send(far, 1)
    second, segments = split(
        [(far_s, [(2, 0, 1, 0, keys)])]
        + pair(y_up, y_up_s, [(2, -4, 0, keys), (0, -8, 0, half)])
        + pair(y_down, y_down_s, [(2, 4, 0, keys), (0, 8, half, half)])
    )
    second_probs, *state = forward(first_key, q, theirs, second, segments, n, keys, state)
    second_tops = state[0]
    last_up, last_down, state = together((last_up, last_down, tuple(state)))
    last = jnp.concatenate([last_up, last_down])
    last, segments = split(
        pair(last, send(last, 1), [(2, -8, 0, half), (2, 8, half, half)])
    )
    weight, hidden, last_kv, last_probs, top, total, attended = project_out(
        first_key, q, state, out_weight, last, segments, n, keys
    )
    predicted, grad_queries = tail(
        weight,
        hidden,
        total,
        attended,
        [up_mine_in, down_mine_in, own_mine, cross],
        [[last_kv], first, second],
        [top, first_tops, second_tops],
        [last_probs, first_probs, second_probs],
    )
    return predicted[None], grad_queries[None]


def solution(mesh):
    placed = (
        P(None, "seq", "tp"),
        P("tp", None),
        P("tp", "seq", None),
        P("tp", "seq", None, None),
        P("tp", "seq"),
        P(),
    )
    return jax.shard_map(
        shards,
        mesh=mesh,
        in_specs=placed,
        out_specs=(P("tp", "seq", None), P("tp", "seq", None)),
        check_vma=False,
    )
```

```python
import functools
import math

import jax
import jax.numpy as jnp
from jax import lax
from jax.experimental import pallas as pl
from jax.experimental.pallas import tpu as pltpu
from jax.sharding import PartitionSpec as P

DT = 8192
QH = 16
KVH = 4
RING = 4
HD = 128
GROUP = QH // KVH
NORM_EPS = 1e-05
MASKED = -1e30
LOWEST = -1e29
SCALE = HD ** (-0.5)
SCALE2 = SCALE * math.log2(math.e)
bf16 = jnp.bfloat16
f32 = jnp.float32


def whole(memory_space=pltpu.VMEM):
    return pl.BlockSpec(memory_space=memory_space)


def params(mebibytes):
    return pltpu.CompilerParams(vmem_limit_bytes=mebibytes * 2**20)


def nt_dot(a, b):
    return lax.dot_general(a, b, (((1,), (1,)), ((), ())), preferred_element_type=f32)


def tn_dot(a, b):
    return lax.dot_general(a, b, (((0,), (0,)), ((), ())), preferred_element_type=f32)


def project_kernel(hops, cuts, _, rows_hbm, weight_hbm, *refs):
    outs, (rows_ref, weight_ref, row_sem, weight_sem) = refs[: len(cuts)], refs[len(cuts) :]
    tokens, width = rows_hbm.shape[1], weight_hbm.shape[1]
    strip = 512
    me = lax.axis_index("tp")
    base = me // RING * RING
    loads = []
    for i, hop in enumerate(hops):
        for z in range(2):
            replica = (base + z * RING) % (2 * RING) + (me + hop) % RING
            k = 2 * i + z
            loads.append(
                pltpu.make_async_copy(
                    rows_hbm.at[replica], rows_ref.at[pl.ds(k * tokens, tokens)], row_sem.at[k]
                )
            )
    strips = [
        pltpu.make_async_copy(
            weight_hbm.at[:, pl.ds(at, strip)], weight_ref.at[:, pl.ds(at, strip)], weight_sem.at[i]
        )
        for i, at in enumerate(range(0, width, strip))
    ]
    for copy in loads + strips:
        copy.start()
    for copy in loads:
        copy.wait()

    def put(block, at):
        size = block.shape[1]
        for out, (replica, count, first, end) in zip(outs, cuts):
            if first <= at < end:
                for z in range(count):
                    row = (replica + z) * tokens
                    out[z, :, at - first : at - first + size] = block[row : row + tokens]

    rows = rows_ref[...]
    for copy, at in zip(strips, range(0, width, strip)):
        copy.wait()
        put(
            jnp.dot(rows, weight_ref[:, at : at + strip], preferred_element_type=f32).astype(bf16),
            at,
        )
    rows32 = rows.astype(f32)
    squares = jnp.sum(rows32 * rows32, axis=-1, keepdims=True)
    high = squares.astype(bf16).astype(f32)
    lane = lax.broadcasted_iota(jnp.int32, (rows.shape[0], 128), 1)
    put(
        jnp.where(lane == me, high, jnp.where(lane == me + 8, squares - high, 0.0)).astype(bf16),
        width,
    )


def project(after, rows, weight, hops, cuts):
    _, tokens, depth = rows.shape
    width = weight.shape[1]
    count = 2 * len(hops)
    return pl.pallas_call(
        functools.partial(project_kernel, hops, cuts),
        in_specs=[whole(pl.ANY)] + [whole(pltpu.HBM)] * 2,
        out_specs=[whole()] * len(cuts),
        out_shape=[
            jax.ShapeDtypeStruct((z, tokens, end - first), bf16) for _, z, first, end in cuts
        ],
        scratch_shapes=[
            pltpu.VMEM((count * tokens, depth), bf16),
            pltpu.VMEM((depth, width), bf16),
            pltpu.SemaphoreType.DMA((count,)),
            pltpu.SemaphoreType.DMA((width // 512,)),
        ],
        compiler_params=params(16),
        cost_estimate=pl.CostEstimate(
            flops=4 * count * tokens * depth * width, bytes_accessed=8 * 2**20, transcendentals=0
        ),
        name="project",
    )(after, rows, weight)


def join_kernel(far_ref, below_ref, above_ref, up_ref, down_ref, both_ref):
    keys = far_ref.shape[0]
    half = keys // 2
    up_ref[:keys] = far_ref[...]
    up_ref[keys:] = below_ref[:half]
    down_ref[:keys] = far_ref[...]
    down_ref[keys:] = above_ref[half:]
    both_ref[:keys] = below_ref[...]
    both_ref[keys:] = above_ref[...]


def join(far, below, above):
    keys, width = far.shape
    rows = (keys + keys // 2, keys + keys // 2, 2 * keys)
    return pl.pallas_call(
        join_kernel,
        in_specs=[whole()] * 3,
        out_specs=[whole()] * 3,
        out_shape=[jax.ShapeDtypeStruct((r, width), bf16) for r in rows],
        compiler_params=params(16),
        name="join",
    )(far, below, above)


def add_kernel(up_in, down_in, *refs):
    ins, outs = refs[:4], refs[4:]
    cut = up_in.shape[-1]
    for z in range(2):
        up, down, up_out, down_out = ins[2 * z], ins[2 * z + 1], outs[2 * z], outs[2 * z + 1]
        up_out[0, :, :cut] = (up[0, :, :cut].astype(f32) + up_in[z].astype(f32)).astype(bf16)
        up_out[0, :, cut:] = up[0, :, cut:]
        down_out[0, :, :cut] = down[0, :, :cut]
        down_out[0, :, cut:] = (down[0, :, cut:].astype(f32) + down_in[z].astype(f32)).astype(bf16)


def add(up_in, down_in, *sums):
    return pl.pallas_call(
        add_kernel,
        in_specs=[whole()] * 6,
        out_specs=[whole()] * 4,
        out_shape=[jax.ShapeDtypeStruct(a.shape, bf16) for a in sums],
        compiler_params=params(16),
        name="add",
    )(up_in, down_in, *sums)


def query_group(q_ref, g):
    return jnp.concatenate(
        [q_ref[:, (GROUP * g + h) * HD : (GROUP * g + h + 1) * HD] for h in range(GROUP)], axis=0
    )


def fill_bias(first_ref, segments, n, shard_keys, bias_ref):
    tokens = bias_ref.shape[1]
    first_key, me = first_ref[0, 0], lax.axis_index("seq")
    first_token = (shard_keys - tokens) * n + me * tokens
    row = 0
    for flip, hop, core, first, rows in segments:
        shard = lax.rem((me ^ flip) + hop, n) ^ core
        key_at = shard * shard_keys + first + lax.broadcasted_iota(jnp.int32, (rows, tokens), 0)
        token_at = first_token + lax.broadcasted_iota(jnp.int32, (rows, tokens), 1)
        bias_ref[row : row + rows, :] = jnp.where(
            (key_at >= first_key) & (key_at <= token_at), 0.0, MASKED
        )
        row += rows


def blocks_of(arrays):
    found, row = [], 0
    for a in arrays:
        rows = a.shape[0]
        step = 256 if rows % 256 == 0 else rows
        for at in range(0, rows, step):
            found.append((a, at, row + at, step))
        row += rows
    return found


def spans_of(arrays):
    found, row = [], 0
    for a in arrays:
        found.append((a, row, a.shape[0]))
        row += a.shape[0]
    return found


def softmax_step(g, q_ref, kv_refs, bias_ref, probs_ref, top, total, acc):
    query = query_group(q_ref, g)

    def score(kv_ref, at, row, rows):
        bias = bias_ref[row : row + rows, :]
        return nt_dot(kv_ref[at : at + rows, g * HD : (g + 1) * HD], query) + jnp.concatenate(
            [bias] * GROUP, axis=1
        )

    new_top = top
    for block in blocks_of(kv_refs):
        new_top = jnp.maximum(new_top, jnp.max(score(*block), axis=0, keepdims=True))
    shift = new_top * SCALE2
    rescale = jnp.exp2(top * SCALE2 - shift)
    total = total * rescale
    acc = acc * rescale
    for block in blocks_of(kv_refs):
        probs = jnp.exp2(score(*block) * SCALE2 - shift)
        total = total + jnp.sum(probs, axis=0, keepdims=True)
        probs_ref[g, block[2] : block[2] + block[3], :] = probs.astype(bf16)
    for kv_ref, row, rows in spans_of(kv_refs):
        acc = acc + tn_dot(
            kv_ref[:, (KVH + g) * HD : (KVH + g + 1) * HD], probs_ref[g, row : row + rows, :]
        )
    return new_top, total, acc


def forward_kernel(segments, n, shard_keys, n_arrays, with_state, *refs):
    first_ref, q_ref = refs[:2]
    kv_refs, refs = refs[3 : 3 + n_arrays], refs[3 + n_arrays :]
    if with_state:
        m_in, l_in, acc_in = refs[:3]
        refs = refs[3:]
    probs_ref, m_out, l_out, acc_out, bias_ref = refs
    span = GROUP * q_ref.shape[0]
    fill_bias(first_ref, segments, n, shard_keys, bias_ref)
    for g in range(KVH):
        cols = slice(g * span, (g + 1) * span)
        if with_state:
            state = m_in[:, cols], l_in[:, cols], acc_in[g]
        else:
            state = (
                jnp.full((1, span), LOWEST, f32),
                jnp.zeros((1, span), f32),
                jnp.zeros((HD, span), f32),
            )
        m_out[:, cols], l_out[:, cols], acc_out[g] = softmax_step(
            g, q_ref, kv_refs, bias_ref, probs_ref, *state
        )


def forward(first_key, q, after, arrays, segments, n, shard_keys, state):
    keys = sum(a.shape[0] for a in arrays)
    tokens = q.shape[0]
    wide = QH * tokens
    span = GROUP * tokens
    state = tuple(state) if state is not None else ()
    return pl.pallas_call(
        functools.partial(
            forward_kernel, tuple(segments), n, shard_keys, len(arrays), bool(state)
        ),
        in_specs=[whole(pltpu.SMEM), whole(), whole(pl.ANY)]
        + [whole()] * (len(arrays) + len(state)),
        out_specs=[whole()] * 4,
        out_shape=[
            jax.ShapeDtypeStruct((KVH, keys, span), bf16),
            jax.ShapeDtypeStruct((1, wide), f32),
            jax.ShapeDtypeStruct((1, wide), f32),
            jax.ShapeDtypeStruct((KVH, HD, span), f32),
        ],
        scratch_shapes=[pltpu.VMEM((keys, tokens), f32)],
        compiler_params=params(14),
        cost_estimate=pl.CostEstimate(
            flops=1000, bytes_accessed=1000, transcendentals=0
        ),
        name="forward",
    )(first_key, q, after, *arrays, *state)


def hidden_kernel(count, segments, n, shard_keys, *refs):
    first_ref, q_ref, m_in, l_in, acc_in, weight_hbm = refs[:6]
    arrays, refs = refs[6 : 6 + count], refs[6 + count :]
    weight_ref, hidden_ref, kv_ref, probs_ref, m_ref, l_ref, turned_ref, bias_ref, sem = refs
    tokens = q_ref.shape[0]
    span = GROUP * tokens
    load = pltpu.make_async_copy(weight_hbm, weight_ref, sem.at[0])
    load.start()
    for a, row, rows in spans_of(arrays):
        kv_ref[row : row + rows] = a[...]
    fill_bias(first_ref, segments, n, shard_keys, bias_ref)
    rows = []
    for g in range(KVH):
        cols = slice(g * span, (g + 1) * span)
        top, total, acc = softmax_step(
            g, q_ref, [kv_ref], bias_ref, probs_ref, m_in[:, cols], l_in[:, cols], acc_in[g]
        )
        m_ref[:, cols] = top
        l_ref[:, cols] = total
        acc = acc / total
        turned_ref[g] = acc
        rows += [acc[:, h * tokens : (h + 1) * tokens].T.astype(bf16) for h in range(GROUP)]
    load.wait()
    hidden_ref[...] = jnp.dot(
        jnp.concatenate(rows, axis=1), weight_ref[...], preferred_element_type=f32
    )


def project_out(first_key, q, state, weight, arrays, segments, n, shard_keys):
    keys = sum(a.shape[0] for a in arrays)
    tokens = q.shape[0]
    wide = QH * tokens
    span = GROUP * tokens
    width = weight.shape[1]
    return pl.pallas_call(
        functools.partial(hidden_kernel, len(arrays), tuple(segments), n, shard_keys),
        in_specs=[whole(pltpu.SMEM)]
        + [whole()] * 4
        + [whole(pltpu.HBM)]
        + [whole()] * len(arrays),
        out_specs=[whole()] * 7,
        out_shape=[
            jax.ShapeDtypeStruct(weight.shape, bf16),
            jax.ShapeDtypeStruct((tokens, width), f32),
            jax.ShapeDtypeStruct((keys, arrays[0].shape[1]), bf16),
            jax.ShapeDtypeStruct((KVH, keys, span), bf16),
            jax.ShapeDtypeStruct((1, wide), f32),
            jax.ShapeDtypeStruct((1, wide), f32),
            jax.ShapeDtypeStruct((KVH, HD, span), f32),
        ],
        scratch_shapes=[pltpu.VMEM((keys, tokens), f32), pltpu.SemaphoreType.DMA((1,))],
        compiler_params=params(14),
        cost_estimate=pl.CostEstimate(
            flops=1000, bytes_accessed=1000, transcendentals=0
        ),
        name="project_out",
    )(first_key, q, *state, weight, *arrays)


def tail_kernel(counts, *refs):
    calls = len(counts)
    weight_ref, hidden_ref, l_ref, attended_ref = refs[:4]
    target_refs, refs = refs[4:8], refs[8:]
    groups = []
    for count in counts:
        groups.append(refs[:count])
        refs = refs[count:]
    tops_refs, probs_refs, refs = refs[:calls], refs[calls : 2 * calls], refs[2 * calls :]
    predicted_ref, out_ref, grad_ref, delta_ref, turned_ref = refs
    m_ref = tops_refs[0]
    tokens = predicted_ref.shape[0]
    width = weight_ref.shape[1]
    span = GROUP * tokens
    hidden = hidden_ref[...]
    inv_rms = lax.rsqrt(jnp.mean(hidden * hidden, axis=-1, keepdims=True) + NORM_EPS)
    scaled = hidden * inv_rms
    predicted_ref[...] = scaled.astype(bf16)
    target = sum(t[0].astype(f32) for t in target_refs)
    squares = jnp.sum(target[:, width:], axis=-1, keepdims=True)
    target = target[:, :width] * lax.rsqrt(squares / DT + NORM_EPS)
    error = scaled - target
    grad = inv_rms * (error - scaled * jnp.mean(error * scaled, axis=-1, keepdims=True))
    grad_turned = nt_dot(weight_ref[...], grad.astype(bf16)).astype(bf16)
    grad_ref[...] = grad_turned
    for head in range(QH):
        g, h = divmod(head, GROUP)
        block = (
            grad_turned[head * HD : (head + 1) * HD].astype(f32)
            * attended_ref[g, :, h * tokens : (h + 1) * tokens]
        )
        delta_ref[:, head * tokens : (head + 1) * tokens] = jnp.sum(block, axis=0, keepdims=True)
    for c, (kv_refs, weights_ref, tops_ref) in enumerate(zip(groups, probs_refs, tops_refs)):
        for g in range(KVH):
            cols = slice(g * span, (g + 1) * span)
            grad_g = jnp.concatenate(
                [
                    grad_ref[(GROUP * g + h) * HD : (GROUP * g + h + 1) * HD, :]
                    for h in range(GROUP)
                ],
                axis=1,
            )
            delta = delta_ref[:, cols]
            part = None
            for keys_ref, row, rows in spans_of(kv_refs):
                slope = jnp.dot(
                    keys_ref[:, (KVH + g) * HD : (KVH + g + 1) * HD],
                    grad_g,
                    preferred_element_type=f32,
                )
                probs = weights_ref[g, row : row + rows, :].astype(f32)
                low = (probs * (slope - delta)).astype(bf16)
                term = tn_dot(keys_ref[:, g * HD : (g + 1) * HD], low)
                part = term if part is None else part + term
            factor = SCALE / l_ref[:, cols]
            if c > 0:
                factor = factor * jnp.exp2((tops_ref[:, cols] - m_ref[:, cols]) * SCALE2)
            part = part * factor
            if c > 0:
                part = part + turned_ref[g]
            if c + 1 < calls:
                turned_ref[g] = part
                continue
            for h in range(GROUP):
                head = GROUP * g + h
                out_ref[:, head * HD : (head + 1) * HD] = part[
                    :, h * tokens : (h + 1) * tokens
                ].T


def tail(weight, hidden, l, attended, targets, groups, tops, probs):
    arrays = [a for g in groups for a in g]
    keys = sum(a.shape[0] for a in arrays)
    tokens, width = hidden.shape
    wide = QH * tokens
    return pl.pallas_call(
        functools.partial(tail_kernel, tuple(len(g) for g in groups)),
        in_specs=[whole()] * (4 + len(targets) + len(arrays) + 2 * len(groups)),
        out_specs=[whole()] * 2,
        out_shape=[
            jax.ShapeDtypeStruct((tokens, width), bf16),
            jax.ShapeDtypeStruct((tokens, QH * HD), f32),
        ],
        scratch_shapes=[
            pltpu.VMEM((QH * HD, tokens), bf16),
            pltpu.VMEM((1, wide), f32),
            pltpu.VMEM((KVH, HD, GROUP * tokens), f32),
        ],
        compiler_params=params(12),
        cost_estimate=pl.CostEstimate(
            flops=8 * keys * wide * HD, bytes_accessed=keys * wide * 2, transcendentals=0
        ),
        name="tail",
    )(weight, hidden, l, attended, *targets, *arrays, *tops, *probs)


def shards(teacher_rows, projection, queries, cache_kv, first_key, out_weight):
    n = lax.axis_size("seq")
    parts = lax.axis_size("tp")
    keys = cache_kv.shape[1]
    half = keys // 2
    width = projection.shape[1]
    wide = width + 128
    cut = width // 2
    together = lax.optimization_barrier

    def send(x, flip, hop=0):
        return lax.ppermute(x, "seq", [(i, ((i ^ flip) + hop) % n) for i in range(n)])

    def send_tp(x, flip, hop=0):
        perm = [(i, (i ^ flip) // RING * RING + (i + hop) % RING) for i in range(parts)]
        return lax.ppermute(x, "tp", perm)

    def pair(x, swapped, runs):
        here = [(flip, hop % n, 0, first, rows) for flip, hop, first, rows in runs]
        there = [(flip, hop % n, 1, first, rows) for flip, hop, first, rows in runs]
        return [(x, here), (swapped, there)]

    def split(call):
        return [a for a, _ in call], [s for _, runs in call for s in runs]

    q = queries[0]
    teacher_rows, projection, out_weight = (
        pltpu.with_memory_space_constraint(a, pltpu.HBM)
        for a in (teacher_rows, projection, out_weight)
    )
    own = cache_kv.reshape(keys, -1)
    far = send(own, 2)
    below = send(own, 0, 4)
    above = send(own, 0, -4)
    own_s = send(own, 1)
    x_up, x_down = project(own_s, teacher_rows, projection, (2,), ((0, 2, 0, cut), (0, 2, cut, wide)))
    x_up_in = send_tp(x_up, 0, 1)
    x_down_in = send_tp(x_down, 0, -1)
    sums = project(x_up, teacher_rows, projection, (1, -1, 0), tuple((i, 1, 0, wide) for i in range(6)))
    far, below, above, sums = together((far, below, above, tuple(sums)))
    up_mine, up_theirs, down_mine, down_theirs, own_mine, own_theirs = sums
    up_two, down_two, near = join(far, below, above)
    y_up = send(up_two, 0, 4)
    y_down = send(down_two, 0, -4)
    near_s = send(near, 1)
    x_up_in, x_down_in, up_two = together((x_up_in, x_down_in, up_two))
    up_mine, down_mine, up_theirs, down_theirs = add(
        x_up_in, x_down_in, up_mine, down_mine, up_theirs, down_theirs
    )
    up_theirs_in = send_tp(up_theirs, 0, 1)
    down_theirs_in = send_tp(down_theirs, 0, -1)
    first, segments = split(
        pair(own, own_s, [(0, 0, 0, keys)])
        + [(far, [(2, 0, 0, 0, keys)])]
        + pair(near, near_s, [(0, -4, 0, keys), (0, 4, 0, keys)])
    )
    first_probs, *state = forward(first_key, q, up_theirs, first, segments, n, keys, None)
    first_tops = state[0]
    y_up, y_down, up_theirs_in, down_theirs_in, up_mine, down_mine, state = together(
        (y_up, y_down, up_theirs_in, down_theirs_in, up_mine, down_mine, tuple(state))
    )
    y_up_s, y_down_s = send(y_up, 1), send(y_down, 1)
    theirs = up_theirs_in.astype(f32) + down_theirs_in.astype(f32) + own_theirs.astype(f32)
    theirs = theirs.astype(bf16)
    cross = send_tp(theirs, RING)
    last_up = send(y_up[:half], 0, 4)
    last_down = send(y_down[half:keys], 0, -4)
    up_mine_in = send_tp(up_mine, 0, 1)
    down_mine_in = send_tp(down_mine, 0, -1)
    second, segments = split(
        pair(y_up, y_up_s, [(2, -4, 0, keys), (0, -8, 0, half)])
        + pair(y_down, y_down_s, [(2, 4, 0, keys), (0, 8, half, half)])
    )
    second_probs, *state = forward(first_key, q, theirs, second, segments, n, keys, state)
    second_tops = state[0]
    last_up, last_down, state = together((last_up, last_down, tuple(state)))
    far, state = together((far, tuple(state)))
    far_s = send(far, 1)
    crossed = send(jnp.concatenate([last_up, last_down]), 1)
    last, segments = split(
        [
            (last_up, [(2, 8, 0, 0, half)]),
            (last_down, [(2, 8, 0, half, half)]),
            (crossed, [(2, 8, 1, 0, half), (2, 8, 1, half, half)]),
            (far_s, [(2, 0, 1, 0, keys)]),
        ]
    )
    weight, hidden, last_kv, last_probs, top, total, attended = project_out(
        first_key, q, state, out_weight, last, segments, n, keys
    )
    predicted, grad_queries = tail(
        weight,
        hidden,
        total,
        attended,
        [up_mine_in, down_mine_in, own_mine, cross],
        [[last_kv], first, second],
        [top, first_tops, second_tops],
        [last_probs, first_probs, second_probs],
    )
    return predicted[None], grad_queries[None]


def solution(mesh):
    placed = (
        P(None, "seq", "tp"),
        P("tp", None),
        P("tp", "seq", None),
        P("tp", "seq", None, None),
        P("tp", "seq"),
        P(),
    )
    return jax.shard_map(
        shards,
        mesh=mesh,
        in_specs=placed,
        out_specs=(P("tp", "seq", None), P("tp", "seq", None)),
        check_vma=False,
    )
```

```python
import functools
import math

import jax
import jax.numpy as jnp
from jax import lax
from jax.experimental import pallas as pl
from jax.experimental.pallas import tpu as pltpu
from jax.sharding import PartitionSpec as P

DT = 8192
QH = 16
KVH = 4
RING = 4
HD = 128
GROUP = QH // KVH
NORM_EPS = 1e-05
MASKED = -1e30
LOWEST = -1e29
SCALE = HD ** (-0.5)
SCALE2 = SCALE * math.log2(math.e)
bf16 = jnp.bfloat16
f32 = jnp.float32


def whole(memory_space=pltpu.VMEM):
    return pl.BlockSpec(memory_space=memory_space)


def params(mebibytes):
    return pltpu.CompilerParams(vmem_limit_bytes=mebibytes * 2**20)


def nt_dot(a, b):
    return lax.dot_general(a, b, (((1,), (1,)), ((), ())), preferred_element_type=f32)


def tn_dot(a, b):
    return lax.dot_general(a, b, (((0,), (0,)), ((), ())), preferred_element_type=f32)


def strip_edges(width):
    cuts = [0, 256] + list(range(512, width + 1, 512))
    return list(zip(cuts[:-1], cuts[1:]))


def project_kernel(hops, cuts, _, rows_hbm, weight_hbm, *refs):
    outs, (rows_ref, weight_ref, row_sem, weight_sem) = refs[: len(cuts)], refs[len(cuts) :]
    tokens, width = rows_hbm.shape[1], weight_hbm.shape[1]
    edges = strip_edges(width)
    me = lax.axis_index("tp")
    base = me // RING * RING
    loads = []
    for i, hop in enumerate(hops):
        for z in range(2):
            replica = (base + z * RING) % (2 * RING) + (me + hop) % RING
            k = 2 * i + z
            loads.append(
                pltpu.make_async_copy(
                    rows_hbm.at[replica], rows_ref.at[pl.ds(k * tokens, tokens)], row_sem.at[k]
                )
            )
    strips = [
        pltpu.make_async_copy(
            weight_hbm.at[:, pl.ds(at, end - at)],
            weight_ref.at[:, pl.ds(at, end - at)],
            weight_sem.at[i],
        )
        for i, (at, end) in enumerate(edges)
    ]
    for copy in loads + strips:
        copy.start()
    for copy in loads:
        copy.wait()

    def put(block, at):
        size = block.shape[1]
        for out, (replica, count, first, end) in zip(outs, cuts):
            if first <= at < end:
                for z in range(count):
                    row = (replica + z) * tokens
                    out[z, :, at - first : at - first + size] = block[row : row + tokens]

    rows = rows_ref[...]
    for copy, (at, end) in zip(strips, edges):
        copy.wait()
        put(
            jnp.dot(rows, weight_ref[:, at:end], preferred_element_type=f32).astype(bf16),
            at,
        )
    rows32 = rows.astype(f32)
    squares = jnp.sum(rows32 * rows32, axis=-1, keepdims=True)
    high = squares.astype(bf16).astype(f32)
    lane = lax.broadcasted_iota(jnp.int32, (rows.shape[0], 128), 1)
    put(
        jnp.where(lane == me, high, jnp.where(lane == me + 8, squares - high, 0.0)).astype(bf16),
        width,
    )


def project(after, rows, weight, hops, cuts):
    _, tokens, depth = rows.shape
    width = weight.shape[1]
    count = 2 * len(hops)
    return pl.pallas_call(
        functools.partial(project_kernel, hops, cuts),
        in_specs=[whole(pl.ANY)] + [whole(pltpu.HBM)] * 2,
        out_specs=[whole()] * len(cuts),
        out_shape=[
            jax.ShapeDtypeStruct((z, tokens, end - first), bf16) for _, z, first, end in cuts
        ],
        scratch_shapes=[
            pltpu.VMEM((count * tokens, depth), bf16),
            pltpu.VMEM((depth, width), bf16),
            pltpu.SemaphoreType.DMA((count,)),
            pltpu.SemaphoreType.DMA((len(strip_edges(width)),)),
        ],
        compiler_params=params(16),
        cost_estimate=pl.CostEstimate(
            flops=4 * count * tokens * depth * width, bytes_accessed=8 * 2**20, transcendentals=0
        ),
        name="project",
    )(after, rows, weight)


def join_kernel(far_ref, below_ref, above_ref, up_ref, down_ref, both_ref):
    keys = far_ref.shape[0]
    half = keys // 2
    up_ref[:keys] = far_ref[...]
    up_ref[keys:] = below_ref[:half]
    down_ref[:keys] = far_ref[...]
    down_ref[keys:] = above_ref[half:]
    both_ref[:keys] = below_ref[...]
    both_ref[keys:] = above_ref[...]


def join(far, below, above):
    keys, width = far.shape
    rows = (keys + keys // 2, keys + keys // 2, 2 * keys)
    return pl.pallas_call(
        join_kernel,
        in_specs=[whole()] * 3,
        out_specs=[whole()] * 3,
        out_shape=[jax.ShapeDtypeStruct((r, width), bf16) for r in rows],
        compiler_params=params(16),
        name="join",
    )(far, below, above)


def add_kernel(up_in, down_in, *refs):
    ins, outs = refs[:4], refs[4:]
    cut = up_in.shape[-1]
    for z in range(2):
        up, down, up_out, down_out = ins[2 * z], ins[2 * z + 1], outs[2 * z], outs[2 * z + 1]
        up_out[0, :, :cut] = (up[0, :, :cut].astype(f32) + up_in[z].astype(f32)).astype(bf16)
        up_out[0, :, cut:] = up[0, :, cut:]
        down_out[0, :, :cut] = down[0, :, :cut]
        down_out[0, :, cut:] = (down[0, :, cut:].astype(f32) + down_in[z].astype(f32)).astype(bf16)


def add(up_in, down_in, *sums):
    return pl.pallas_call(
        add_kernel,
        in_specs=[whole()] * 6,
        out_specs=[whole()] * 4,
        out_shape=[jax.ShapeDtypeStruct(a.shape, bf16) for a in sums],
        compiler_params=params(16),
        name="add",
    )(up_in, down_in, *sums)


def query_group(q_ref, g):
    return jnp.concatenate(
        [q_ref[:, (GROUP * g + h) * HD : (GROUP * g + h + 1) * HD] for h in range(GROUP)], axis=0
    )


def fill_bias(first_ref, segments, n, shard_keys, bias_ref):
    tokens = bias_ref.shape[1]
    first_key, me = first_ref[0, 0], lax.axis_index("seq")
    first_token = (shard_keys - tokens) * n + me * tokens
    row = 0
    for flip, hop, core, first, rows in segments:
        shard = lax.rem((me ^ flip) + hop, n) ^ core
        key_at = shard * shard_keys + first + lax.broadcasted_iota(jnp.int32, (rows, tokens), 0)
        token_at = first_token + lax.broadcasted_iota(jnp.int32, (rows, tokens), 1)
        bias_ref[row : row + rows, :] = jnp.where(
            (key_at >= first_key) & (key_at <= token_at), 0.0, MASKED
        )
        row += rows


def blocks_of(arrays):
    found, row = [], 0
    for a in arrays:
        rows = a.shape[0]
        step = 256 if rows % 256 == 0 else rows
        for at in range(0, rows, step):
            found.append((a, at, row + at, step))
        row += rows
    return found


def spans_of(arrays):
    found, row = [], 0
    for a in arrays:
        found.append((a, row, a.shape[0]))
        row += a.shape[0]
    return found


def softmax_step(g, q_ref, kv_refs, bias_ref, probs_ref, top, total, acc):
    query = query_group(q_ref, g)

    def score(kv_ref, at, row, rows):
        bias = bias_ref[row : row + rows, :]
        return nt_dot(kv_ref[at : at + rows, g * HD : (g + 1) * HD], query) + jnp.concatenate(
            [bias] * GROUP, axis=1
        )

    new_top = top
    for block in blocks_of(kv_refs):
        new_top = jnp.maximum(new_top, jnp.max(score(*block), axis=0, keepdims=True))
    shift = new_top * SCALE2
    rescale = jnp.exp2(top * SCALE2 - shift)
    total = total * rescale
    acc = acc * rescale
    for block in blocks_of(kv_refs):
        probs = jnp.exp2(score(*block) * SCALE2 - shift)
        total = total + jnp.sum(probs, axis=0, keepdims=True)
        probs_ref[g, block[2] : block[2] + block[3], :] = probs.astype(bf16)
    for kv_ref, row, rows in spans_of(kv_refs):
        acc = acc + tn_dot(
            kv_ref[:, (KVH + g) * HD : (KVH + g + 1) * HD], probs_ref[g, row : row + rows, :]
        )
    return new_top, total, acc


def forward_kernel(segments, n, shard_keys, n_arrays, with_state, *refs):
    first_ref, q_ref = refs[:2]
    kv_refs, refs = refs[3 : 3 + n_arrays], refs[3 + n_arrays :]
    if with_state:
        m_in, l_in, acc_in = refs[:3]
        refs = refs[3:]
    probs_ref, m_out, l_out, acc_out, bias_ref = refs
    span = GROUP * q_ref.shape[0]
    fill_bias(first_ref, segments, n, shard_keys, bias_ref)
    for g in range(KVH):
        cols = slice(g * span, (g + 1) * span)
        if with_state:
            state = m_in[:, cols], l_in[:, cols], acc_in[g]
        else:
            state = (
                jnp.full((1, span), LOWEST, f32),
                jnp.zeros((1, span), f32),
                jnp.zeros((HD, span), f32),
            )
        m_out[:, cols], l_out[:, cols], acc_out[g] = softmax_step(
            g, q_ref, kv_refs, bias_ref, probs_ref, *state
        )


def forward(first_key, q, after, arrays, segments, n, shard_keys, state):
    keys = sum(a.shape[0] for a in arrays)
    tokens = q.shape[0]
    wide = QH * tokens
    span = GROUP * tokens
    state = tuple(state) if state is not None else ()
    return pl.pallas_call(
        functools.partial(
            forward_kernel, tuple(segments), n, shard_keys, len(arrays), bool(state)
        ),
        in_specs=[whole(pltpu.SMEM), whole(), whole(pl.ANY)]
        + [whole()] * (len(arrays) + len(state)),
        out_specs=[whole()] * 4,
        out_shape=[
            jax.ShapeDtypeStruct((KVH, keys, span), bf16),
            jax.ShapeDtypeStruct((1, wide), f32),
            jax.ShapeDtypeStruct((1, wide), f32),
            jax.ShapeDtypeStruct((KVH, HD, span), f32),
        ],
        scratch_shapes=[pltpu.VMEM((keys, tokens), f32)],
        compiler_params=params(14),
        cost_estimate=pl.CostEstimate(
            flops=1000, bytes_accessed=1000, transcendentals=0
        ),
        name="forward",
    )(first_key, q, after, *arrays, *state)


def hidden_kernel(count, segments, n, shard_keys, *refs):
    first_ref, q_ref, m_in, l_in, acc_in, weight_hbm = refs[:6]
    arrays, refs = refs[6 : 6 + count], refs[6 + count :]
    weight_ref, hidden_ref, kv_ref, probs_ref, m_ref, l_ref, turned_ref, bias_ref, sem = refs
    tokens = q_ref.shape[0]
    span = GROUP * tokens
    load = pltpu.make_async_copy(weight_hbm, weight_ref, sem.at[0])
    load.start()
    for a, row, rows in spans_of(arrays):
        kv_ref[row : row + rows] = a[...]
    fill_bias(first_ref, segments, n, shard_keys, bias_ref)
    rows = []
    for g in range(KVH):
        cols = slice(g * span, (g + 1) * span)
        top, total, acc = softmax_step(
            g, q_ref, [kv_ref], bias_ref, probs_ref, m_in[:, cols], l_in[:, cols], acc_in[g]
        )
        m_ref[:, cols] = top
        l_ref[:, cols] = total
        acc = acc / total
        turned_ref[g] = acc
        rows += [acc[:, h * tokens : (h + 1) * tokens].T.astype(bf16) for h in range(GROUP)]
    load.wait()
    hidden_ref[...] = jnp.dot(
        jnp.concatenate(rows, axis=1), weight_ref[...], preferred_element_type=f32
    )


def project_out(first_key, q, state, weight, arrays, segments, n, shard_keys):
    keys = sum(a.shape[0] for a in arrays)
    tokens = q.shape[0]
    wide = QH * tokens
    span = GROUP * tokens
    width = weight.shape[1]
    return pl.pallas_call(
        functools.partial(hidden_kernel, len(arrays), tuple(segments), n, shard_keys),
        in_specs=[whole(pltpu.SMEM)]
        + [whole()] * 4
        + [whole(pltpu.HBM)]
        + [whole()] * len(arrays),
        out_specs=[whole()] * 7,
        out_shape=[
            jax.ShapeDtypeStruct(weight.shape, bf16),
            jax.ShapeDtypeStruct((tokens, width), f32),
            jax.ShapeDtypeStruct((keys, arrays[0].shape[1]), bf16),
            jax.ShapeDtypeStruct((KVH, keys, span), bf16),
            jax.ShapeDtypeStruct((1, wide), f32),
            jax.ShapeDtypeStruct((1, wide), f32),
            jax.ShapeDtypeStruct((KVH, HD, span), f32),
        ],
        scratch_shapes=[pltpu.VMEM((keys, tokens), f32), pltpu.SemaphoreType.DMA((1,))],
        compiler_params=params(14),
        cost_estimate=pl.CostEstimate(
            flops=1000, bytes_accessed=1000, transcendentals=0
        ),
        name="project_out",
    )(first_key, q, *state, weight, *arrays)


def tail_kernel(counts, *refs):
    calls = len(counts)
    weight_ref, hidden_ref, l_ref, attended_ref = refs[:4]
    target_refs, refs = refs[4:8], refs[8:]
    groups = []
    for count in counts:
        groups.append(refs[:count])
        refs = refs[count:]
    tops_refs, probs_refs, refs = refs[:calls], refs[calls : 2 * calls], refs[2 * calls :]
    predicted_ref, out_ref, grad_ref, delta_ref, turned_ref = refs
    m_ref = tops_refs[0]
    tokens = predicted_ref.shape[0]
    width = weight_ref.shape[1]
    span = GROUP * tokens
    hidden = hidden_ref[...]
    inv_rms = lax.rsqrt(jnp.mean(hidden * hidden, axis=-1, keepdims=True) + NORM_EPS)
    scaled = hidden * inv_rms
    predicted_ref[...] = scaled.astype(bf16)
    target = sum(t[0].astype(f32) for t in target_refs)
    squares = jnp.sum(target[:, width:], axis=-1, keepdims=True)
    target = target[:, :width] * lax.rsqrt(squares / DT + NORM_EPS)
    error = scaled - target
    grad = inv_rms * (error - scaled * jnp.mean(error * scaled, axis=-1, keepdims=True))
    grad_turned = nt_dot(weight_ref[...], grad.astype(bf16)).astype(bf16)
    grad_ref[...] = grad_turned
    for head in range(QH):
        g, h = divmod(head, GROUP)
        block = (
            grad_turned[head * HD : (head + 1) * HD].astype(f32)
            * attended_ref[g, :, h * tokens : (h + 1) * tokens]
        )
        delta_ref[:, head * tokens : (head + 1) * tokens] = jnp.sum(block, axis=0, keepdims=True)
    for c, (kv_refs, weights_ref, tops_ref) in enumerate(zip(groups, probs_refs, tops_refs)):
        for g in range(KVH):
            cols = slice(g * span, (g + 1) * span)
            grad_g = jnp.concatenate(
                [
                    grad_ref[(GROUP * g + h) * HD : (GROUP * g + h + 1) * HD, :]
                    for h in range(GROUP)
                ],
                axis=1,
            )
            delta = delta_ref[:, cols]
            part = None
            for keys_ref, row, rows in spans_of(kv_refs):
                slope = jnp.dot(
                    keys_ref[:, (KVH + g) * HD : (KVH + g + 1) * HD],
                    grad_g,
                    preferred_element_type=f32,
                )
                probs = weights_ref[g, row : row + rows, :].astype(f32)
                low = (probs * (slope - delta)).astype(bf16)
                term = tn_dot(keys_ref[:, g * HD : (g + 1) * HD], low)
                part = term if part is None else part + term
            factor = SCALE / l_ref[:, cols]
            if c > 0:
                factor = factor * jnp.exp2((tops_ref[:, cols] - m_ref[:, cols]) * SCALE2)
            part = part * factor
            if c > 0:
                part = part + turned_ref[g]
            if c + 1 < calls:
                turned_ref[g] = part
                continue
            for h in range(GROUP):
                head = GROUP * g + h
                out_ref[:, head * HD : (head + 1) * HD] = part[
                    :, h * tokens : (h + 1) * tokens
                ].T


def tail(weight, hidden, l, attended, targets, groups, tops, probs):
    arrays = [a for g in groups for a in g]
    keys = sum(a.shape[0] for a in arrays)
    tokens, width = hidden.shape
    wide = QH * tokens
    return pl.pallas_call(
        functools.partial(tail_kernel, tuple(len(g) for g in groups)),
        in_specs=[whole()] * (4 + len(targets) + len(arrays) + 2 * len(groups)),
        out_specs=[whole()] * 2,
        out_shape=[
            jax.ShapeDtypeStruct((tokens, width), bf16),
            jax.ShapeDtypeStruct((tokens, QH * HD), f32),
        ],
        scratch_shapes=[
            pltpu.VMEM((QH * HD, tokens), bf16),
            pltpu.VMEM((1, wide), f32),
            pltpu.VMEM((KVH, HD, GROUP * tokens), f32),
        ],
        compiler_params=params(12),
        cost_estimate=pl.CostEstimate(
            flops=8 * keys * wide * HD, bytes_accessed=keys * wide * 2, transcendentals=0
        ),
        name="tail",
    )(weight, hidden, l, attended, *targets, *arrays, *tops, *probs)


def shards(teacher_rows, projection, queries, cache_kv, first_key, out_weight):
    n = lax.axis_size("seq")
    parts = lax.axis_size("tp")
    keys = cache_kv.shape[1]
    half = keys // 2
    width = projection.shape[1]
    wide = width + 128
    cut = width // 2
    together = lax.optimization_barrier

    def send(x, flip, hop=0):
        return lax.ppermute(x, "seq", [(i, ((i ^ flip) + hop) % n) for i in range(n)])

    def send_tp(x, flip, hop=0):
        perm = [(i, (i ^ flip) // RING * RING + (i + hop) % RING) for i in range(parts)]
        return lax.ppermute(x, "tp", perm)

    def pair(x, swapped, runs):
        here = [(flip, hop % n, 0, first, rows) for flip, hop, first, rows in runs]
        there = [(flip, hop % n, 1, first, rows) for flip, hop, first, rows in runs]
        return [(x, here), (swapped, there)]

    def split(call):
        return [a for a, _ in call], [s for _, runs in call for s in runs]

    q = queries[0]
    teacher_rows, projection, out_weight = (
        pltpu.with_memory_space_constraint(a, pltpu.HBM)
        for a in (teacher_rows, projection, out_weight)
    )
    own = cache_kv.reshape(keys, -1)
    far = send(own, 2)
    below = send(own, 0, 4)
    above = send(own, 0, -4)
    own_s = send(own, 1)
    x_up, x_down = project(own_s, teacher_rows, projection, (2,), ((0, 2, 0, cut), (0, 2, cut, wide)))
    x_up_in = send_tp(x_up, 0, 1)
    x_down_in = send_tp(x_down, 0, -1)
    sums = project(x_up, teacher_rows, projection, (1, -1, 0), tuple((i, 1, 0, wide) for i in range(6)))
    far, below, above, sums = together((far, below, above, tuple(sums)))
    up_mine, up_theirs, down_mine, down_theirs, own_mine, own_theirs = sums
    up_two, down_two, near = join(far, below, above)
    y_up = send(up_two, 0, 4)
    y_down = send(down_two, 0, -4)
    near_s = send(near, 1)
    x_up_in, x_down_in, up_two = together((x_up_in, x_down_in, up_two))
    up_mine, down_mine, up_theirs, down_theirs = add(
        x_up_in, x_down_in, up_mine, down_mine, up_theirs, down_theirs
    )
    up_theirs_in = send_tp(up_theirs, 0, 1)
    down_theirs_in = send_tp(down_theirs, 0, -1)
    first, segments = split(
        pair(own, own_s, [(0, 0, 0, keys)])
        + [(far, [(2, 0, 0, 0, keys)])]
        + pair(near, near_s, [(0, -4, 0, keys), (0, 4, 0, keys)])
    )
    first_probs, *state = forward(first_key, q, up_theirs, first, segments, n, keys, None)
    first_tops = state[0]
    y_up, y_down, up_theirs_in, down_theirs_in, up_mine, down_mine, state = together(
        (y_up, y_down, up_theirs_in, down_theirs_in, up_mine, down_mine, tuple(state))
    )
    y_up_s, y_down_s = send(y_up, 1), send(y_down, 1)
    theirs = up_theirs_in.astype(f32) + down_theirs_in.astype(f32) + own_theirs.astype(f32)
    theirs = theirs.astype(bf16)
    cross = send_tp(theirs, RING)
    last_up = send(y_up[:half], 0, 4)
    last_down = send(y_down[half:keys], 0, -4)
    up_mine_in = send_tp(up_mine, 0, 1)
    down_mine_in = send_tp(down_mine, 0, -1)
    second, segments = split(
        pair(y_up, y_up_s, [(2, -4, 0, keys), (0, -8, 0, half)])
        + pair(y_down, y_down_s, [(2, 4, 0, keys), (0, 8, half, half)])
    )
    second_probs, *state = forward(first_key, q, theirs, second, segments, n, keys, state)
    second_tops = state[0]
    last_up, last_down, state = together((last_up, last_down, tuple(state)))
    far, state = together((far, tuple(state)))
    far_s = send(far, 1)
    crossed = send(jnp.concatenate([last_up, last_down]), 1)
    last, segments = split(
        [
            (last_up, [(2, 8, 0, 0, half)]),
            (last_down, [(2, 8, 0, half, half)]),
            (crossed, [(2, 8, 1, 0, half), (2, 8, 1, half, half)]),
            (far_s, [(2, 0, 1, 0, keys)]),
        ]
    )
    weight, hidden, last_kv, last_probs, top, total, attended = project_out(
        first_key, q, state, out_weight, last, segments, n, keys
    )
    predicted, grad_queries = tail(
        weight,
        hidden,
        total,
        attended,
        [up_mine_in, down_mine_in, own_mine, cross],
        [[last_kv], first, second],
        [top, first_tops, second_tops],
        [last_probs, first_probs, second_probs],
    )
    return predicted[None], grad_queries[None]


def solution(mesh):
    placed = (
        P(None, "seq", "tp"),
        P("tp", None),
        P("tp", "seq", None),
        P("tp", "seq", None, None),
        P("tp", "seq"),
        P(),
    )
    return jax.shard_map(
        shards,
        mesh=mesh,
        in_specs=placed,
        out_specs=(P("tp", "seq", None), P("tp", "seq", None)),
        check_vma=False,
    )
```
